32 devices in a mesh: gx: 4 (over y, core), gy: 8 (over z, x).
Axes of the slice: x: 2, y: 2, z: 4, core: 2. Of those that a mesh axis runs over, the one named last changes fastest.
Arguments:
- initial_warmth: float32 [128, 128, 256], P('gx', 'gy'), may hold values from -4 to 4
- energy_source_density: float32 [128, 128, 256], P('gx', 'gy'), may hold values from -4 to 4
- baseline_transport_coefficient: float32 [128, 128, 256], P('gx', 'gy'), may hold values from 256 to 1024
Outputs:
- new_temperature: float32 [128, 128, 256], P('gx', 'gy')
The draws below stay inside these ranges and needn't reach their ends.
All inputs are finite; a program needn't handle non-finite values.
Results may differ from the reference program's by a relative error of at most 0.0003.
Values sent between devices are 32-bit elements; how exact they have to be, the bound alone decides.
A program may use at most 128 MiB of HBM per device.

```python
import math
import jax
import jax.numpy as jnp
from jax import lax

MESH_COUNT_LAST = 256
MESH_COUNT_LEAD = 128
MESH_COUNT_MIDDLE = 128


def draw_energy_source_density(key, part):
    return jnp.clip(jax.random.normal(key, (MESH_COUNT_LEAD, MESH_COUNT_MIDDLE, MESH_COUNT_LAST), jnp.float32), -4.0, 4.0)


def block_levels(own_key, dims, shards, least, top_value):
    def one(axis_at, parts):
        heights = jax.random.uniform(jax.random.fold_in(jax.random.fold_in(own_key, 6), axis_at), (parts,), jnp.float32, least / len(shards), top_value / len(shards))
        return jnp.repeat(jnp.exp(heights), dims[axis_at] // parts).reshape((-1,) + (1,) * (len(dims) - axis_at - 1))

    loudness = one(*shards[0])
    for cut in shards[1:]:
        loudness = loudness * one(*cut)
    return loudness


def bell_draw(rng, dims, scale, most, cuts=(), held_as=jnp.bfloat16):
    level = block_levels(rng, dims, cuts, -0.22, 0.18) if cuts else 1.0
    array = jax.random.normal(rng, dims, jnp.float32) * scale * level
    return jnp.minimum(jnp.maximum(array, -most), most).astype(held_as)


def setup_inputs(seed: int = 0) -> dict:
    splits = jax.random.split(jax.random.key(seed), 4)
    return {
        "initial_warmth": bell_draw(splits[0], (MESH_COUNT_LEAD, MESH_COUNT_MIDDLE, MESH_COUNT_LAST), 1.0, 4.0, ((0, 4), (1, 8)), jnp.float32),
        "energy_source_density": draw_energy_source_density(jax.random.fold_in(splits[3], 71), 0),
        "baseline_transport_coefficient": jnp.clip(jnp.exp(math.log(1024.0) - 1.3862944 * jax.random.uniform(splits[2], (MESH_COUNT_LEAD, MESH_COUNT_MIDDLE, MESH_COUNT_LAST), jnp.float32) ** block_levels(splits[2], (MESH_COUNT_LEAD, MESH_COUNT_MIDDLE, MESH_COUNT_LAST), ((0, 4), (1, 8)), -0.2, 0.2)), 256.0, 1024.0),
    }


time_step = 1.0
implicit_weight = 0.5

def line_solve(sub_diag, main_diag, super_diag, right_side, line_dim):
    sub_moved = jnp.moveaxis(sub_diag, line_dim, -1)
    main_moved = jnp.moveaxis(main_diag, line_dim, -1)
    super_moved = jnp.moveaxis(super_diag, line_dim, -1)
    right_moved = jnp.moveaxis(right_side, line_dim, -1)
    sub_moved = sub_moved.at[..., 0].set(0.0)
    super_moved = super_moved.at[..., -1].set(0.0)
    solved = lax.linalg.tridiagonal_solve(sub_moved, main_moved, super_moved, right_moved[..., None])[..., 0]
    return jnp.moveaxis(solved, -1, line_dim)

def reference(initial_warmth, energy_source_density, baseline_transport_coefficient):
    warmth_transport_coefficient = baseline_transport_coefficient * (1.0 + 0.5 * initial_warmth * initial_warmth)
    bordered_warmth_values = jnp.pad(initial_warmth, 1)
    cond_pad = jnp.pad(warmth_transport_coefficient, 1)
    leading_direction_boundary = 0.5 * (cond_pad[1:, 1:-1, 1:-1] + cond_pad[:-1, 1:-1, 1:-1])
    middle_direction_boundary = 0.5 * (cond_pad[1:-1, 1:, 1:-1] + cond_pad[1:-1, :-1, 1:-1])
    trailing_direction_boundary = 0.5 * (cond_pad[1:-1, 1:-1, 1:] + cond_pad[1:-1, 1:-1, :-1])
    summed_energy_current = leading_direction_boundary[1:] * (bordered_warmth_values[2:, 1:-1, 1:-1] - initial_warmth) - leading_direction_boundary[:-1] * (initial_warmth - bordered_warmth_values[:-2, 1:-1, 1:-1])
    summed_energy_current = summed_energy_current + middle_direction_boundary[:, 1:] * (bordered_warmth_values[1:-1, 2:, 1:-1] - initial_warmth) - middle_direction_boundary[:, :-1] * (initial_warmth - bordered_warmth_values[1:-1, :-2, 1:-1])
    summed_energy_current = summed_energy_current + trailing_direction_boundary[:, :, 1:] * (bordered_warmth_values[1:-1, 1:-1, 2:] - initial_warmth) - trailing_direction_boundary[:, :, :-1] * (initial_warmth - bordered_warmth_values[1:-1, 1:-1, :-2])
    increment = time_step * (summed_energy_current + energy_source_density)
    weight = implicit_weight * time_step
    step_x = line_solve(-weight * leading_direction_boundary[:-1], 1.0 + weight * (leading_direction_boundary[:-1] + leading_direction_boundary[1:]), -weight * leading_direction_boundary[1:], increment, 0)
    step_y = line_solve(-weight * middle_direction_boundary[:, :-1], 1.0 + weight * (middle_direction_boundary[:, :-1] + middle_direction_boundary[:, 1:]), -weight * middle_direction_boundary[:, 1:], step_x, 1)
    trailing_direction_update = line_solve(-weight * trailing_direction_boundary[:, :, :-1], 1.0 + weight * (trailing_direction_boundary[:, :, :-1] + trailing_direction_boundary[:, :, 1:]), -weight * trailing_direction_boundary[:, :, 1:], step_y, 2)
    return initial_warmth + trailing_direction_update
```

```python
import functools

import jax
import jax.numpy as jnp
from jax import lax
from jax.experimental import pallas as pl
from jax.experimental.pallas import tpu as pltpu
from jax.sharding import PartitionSpec as P

MESH = pl.DeviceIdType.MESH
LANES = 128


def kernel(nx, ny, gx, gy, lx, ly, u_hbm, s_hbm, k_hbm, o_hbm,
           field, rhs, xd, xe, xw, yd, ye, yw, yi, hx, hys, hyr,
           zq, zfm, zfp,
           xsend, xrecv, xback, xgot, ycs, ycr, yrs, yrr, yback, ygot, yfw, yfi,
           in_sem, out_sem, hs_sem, hr_sem, xs_sem, xr_sem, xbs_sem, xbr_sem,
           ycs_sem, ycr_sem, yrs_sem, yrr_sem, ybs_sem, ybr_sem):
    rows = nx * ny
    mx = lax.axis_index("gx")
    my = lax.axis_index("gy")

    loads = []
    for a, (src, dst) in enumerate(((u_hbm, field.at[0]), (k_hbm, field.at[1]), (s_hbm, rhs))):
        for h in range(2):
            c = pltpu.make_async_copy(src.at[:, pl.ds(h * LANES, LANES)], dst.at[h], in_sem.at[a, h])
            c.start()
            loads.append(c)

    barrier = pltpu.get_barrier_semaphore()
    for o in range(1, gx):
        pl.semaphore_signal(barrier, inc=1, device_id={"gx": lax.rem(mx + o, gx)}, device_id_type=MESH)
    for o in range(1, gy):
        pl.semaphore_signal(barrier, inc=1, device_id={"gy": lax.rem(my + o, gy)}, device_id_type=MESH)

    for c in loads[:4]:
        c.wait()
    block = 32
    for r in range(0, rows, block):
        u = field[0, :, r:r + block, :]
        field[1, :, r:r + block, :] = field[1, :, r:r + block, :] * (1.0 + 0.5 * u * u)

    def yrow(q, j):
        return [field[q, h, pl.ds(j, nx, stride=ny), :] for h in range(2)]

    for q in range(2):
        for h in range(2):
            hys[0, q, h] = field[q, h, pl.ds(0, nx, stride=ny), :]
            hys[1, q, h] = field[q, h, pl.ds(ny - 1, nx, stride=ny), :]

    pl.semaphore_wait(barrier, gx + gy - 2)

    def halo(axis, me, count, src_first, src_last, recv, base):
        down = pltpu.make_async_remote_copy(
            src_ref=src_first, dst_ref=recv.at[1], send_sem=hs_sem.at[base], recv_sem=hr_sem.at[base],
            device_id={axis: lax.rem(me + count - 1, count)}, device_id_type=MESH)
        up = pltpu.make_async_remote_copy(
            src_ref=src_last, dst_ref=recv.at[0], send_sem=hs_sem.at[base + 1], recv_sem=hr_sem.at[base + 1],
            device_id={axis: lax.rem(me + 1, count)}, device_id_type=MESH)

        @pl.when(me > 0)
        def _():
            down.start()

        @pl.when(me < count - 1)
        def _():
            up.start()

        @pl.when(me == 0)
        def _():
            recv[0] = jnp.zeros(recv.shape[1:], jnp.float32)

        @pl.when(me == count - 1)
        def _():
            recv[1] = jnp.zeros(recv.shape[1:], jnp.float32)

        def wait():
            @pl.when(me > 0)
            def _():
                down.wait_send()
                up.wait_recv()

            @pl.when(me < count - 1)
            def _():
                up.wait_send()
                down.wait_recv()
        return wait

    wait_y = halo("gy", my, gy, hys.at[0], hys.at[1], hyr, 0)
    wait_x = halo("gx", mx, gx, field.at[:, :, pl.ds(0, ny), :],
                  field.at[:, :, pl.ds(rows - ny, ny), :], hx, 2)

    for c in loads[4:]:
        c.wait()

    lane = lax.broadcasted_iota(jnp.int32, (block, LANES), 1)

    def prev(a, s):
        if s == LANES:
            return a[1], a[0]
        p0, p1 = pltpu.roll(a[0], s, 1), pltpu.roll(a[1], s, 1)
        return p0, jnp.where(lane < s, p0, p1)

    def nxt(a, s):
        n0, n1 = pltpu.roll(a[0], LANES - s, 1), pltpu.roll(a[1], LANES - s, 1)
        return jnp.where(lane >= LANES - s, n1, n0), n1

    first, last = lane == 0, lane == LANES - 1

    for r in range(0, rows, block):
        at = pl.ds(r, block)
        u = [field[0, h, at, :] for h in range(2)]
        c = [field[1, h, at, :] for h in range(2)]
        up_, cp = prev(u, 1), prev(c, 1)
        un, cn = nxt(u, 1), nxt(c, 1)
        zero = jnp.zeros_like(lane, jnp.float32)
        up_, cp = [jnp.where(first, zero, up_[0]), up_[1]], [jnp.where(first, zero, cp[0]), cp[1]]
        un, cn = [un[0], jnp.where(last, zero, un[1])], [cn[0], jnp.where(last, zero, cn[1])]
        for h in range(2):
            gm, gp = 0.25 * (c[h] + cp[h]), 0.25 * (c[h] + cn[h])
            rhs[h, at, :] = rhs[h, at, :] + 2.0 * (gp * (un[h] - u[h]) - gm * (u[h] - up_[h]))
            if h == 0:
                zq[0, h, at, :] = jnp.where(first, zero, gm)
                zq[1, h, at, :] = gp
                zq[2, h, at, :] = jnp.where(first, 1.0 + gm, 1.0)
            else:
                zq[0, h, at, :] = gm
                zq[1, h, at, :] = jnp.where(last, zero, gp)
                zq[2, h, at, :] = jnp.where(last, 1.0 + gp, 1.0)

    def zfactor(step):
        s = 1 << step
        for r in range(0, rows, block):
            at = pl.ds(r, block)
            qm = [zq[0, h, at, :] for h in range(2)]
            qp = [zq[1, h, at, :] for h in range(2)]
            m = [zq[2, h, at, :] for h in range(2)]
            ib = [1.0 / (m[h] + (qm[h] + qp[h])) for h in range(2)]
            if s == LANES:
                fp0, fm1 = qp[0] * ib[1], qm[1] * ib[0]
                zfm[step, 0, at, :] = fp0
                zfm[step, 1, at, :] = fm1
                zfp[step, 0, at, :] = 1.0 / (m[0] + fp0 * m[1])
                zfp[step, 1, at, :] = 1.0 / (m[1] + fm1 * m[0])
                continue
            ip, inx = prev(ib, s), nxt(ib, s)
            mp, mn = prev(m, s), nxt(m, s)
            qmp, qpn = prev(qm, s), nxt(qp, s)
            for h in range(2):
                fm, fp = qm[h] * ip[h], qp[h] * inx[h]
                zfm[step, h, at, :] = fm
                zfp[step, h, at, :] = fp
                zq[0, h, at, :] = fm * qmp[h]
                zq[1, h, at, :] = fp * qpn[h]
                zq[2, h, at, :] = m[h] + (fm * mp[h] + fp * mn[h])

    wait_y()

    def joined(parts):
        return jnp.concatenate(parts, axis=0)

    up_, cp = joined([hyr[0, 0, 0], hyr[0, 0, 1]]), joined([hyr[0, 1, 0], hyr[0, 1, 1]])
    u, c = joined(yrow(0, 0)), joined(yrow(1, 0))
    gm = 0.25 * (c + cp)
    for j in range(ny):
        if j < ny - 1:
            un, cn = joined(yrow(0, j + 1)), joined(yrow(1, j + 1))
        else:
            un, cn = joined([hyr[1, 0, 0], hyr[1, 0, 1]]), joined([hyr[1, 1, 0], hyr[1, 1, 1]])
        gp = 0.25 * (c + cn)
        t = 2.0 * (gp * (un - u) - gm * (u - up_))
        yw[j] = gm
        if j == ny - 1:
            yw[ny] = gp
        for h in range(2):
            at = pl.ds(j, nx, stride=ny)
            rhs[h, at, :] = rhs[h, at, :] + t[h * nx:(h + 1) * nx]
        up_, u, c, gm = u, un, cn, gp

    wait_x()

    def xrow(q, i):
        return joined([field[q, h, pl.ds(i * ny, ny), :] for h in range(2)])

    def split_send(values, buf, count, per):
        for q, v in enumerate(values):
            for t in range(count):
                buf[t, q] = v[t * per:(t + 1) * per]

    up_, cp = joined([hx[0, 0, 0], hx[0, 0, 1]]), joined([hx[0, 1, 0], hx[0, 1, 1]])
    u, c = xrow(0, 0), xrow(1, 0)
    gm = 0.25 * (c + cp)
    edge_lo = jnp.where(mx == 0, 1.0, 0.0)
    edge_hi = jnp.where(mx == gx - 1, 1.0, 0.0)
    mass, link, dd, sig, d1 = None, None, None, None, None
    for i in range(nx):
        if i < nx - 1:
            un, cn = xrow(0, i + 1), xrow(1, i + 1)
        else:
            un, cn = joined([hx[1, 0, 0], hx[1, 0, 1]]), joined([hx[1, 1, 0], hx[1, 1, 1]])
        gp = 0.25 * (c + cn)
        d = joined([rhs[h, pl.ds(i * ny, ny), :] for h in range(2)])
        d = d + 2.0 * (gp * (un - u) - gm * (u - up_))
        if i == 0:
            mass, link, dd = 1.0 + edge_lo * gm, (1.0 - edge_lo) * gm, d
        else:
            mass, link, dd = 1.0 + w * mass, w * link, d + w * dd
        if i < nx - 1:
            ib = 1.0 / (mass + link + gp)
            w = gp * ib
            e = link * ib
            xd[i], xe[i], xw[i] = dd * ib, e, w
            sig = e * mass if i == 0 else sig + e * mass
            d1 = e * dd if i == 0 else d1 + e * dd
        up_, u, c, gm = u, un, cn, gp
    mass = mass + edge_hi * gm
    split_send((link, mass, sig, dd, d1), xsend, gx, lx)

    def exchange(axis, me, count, src, dst, send_sem, recv_sem):
        copies = []
        for o in range(1, count):
            peer = lax.rem(me + o, count)
            c = pltpu.make_async_remote_copy(
                src_ref=src.at[peer], dst_ref=dst.at[me], send_sem=send_sem.at[o], recv_sem=recv_sem.at[o],
                device_id={axis: peer}, device_id_type=MESH)
            c.start()
            copies.append(c)
        dst[me] = src[me]

        def wait():
            for o in range(1, count):
                origin = lax.rem(me + count - o, count)
                c = pltpu.make_async_remote_copy(
                    src_ref=src.at[origin], dst_ref=dst.at[origin], send_sem=send_sem.at[o],
                    recv_sem=recv_sem.at[o], device_id={axis: origin}, device_id_type=MESH)
                c.wait_recv()
            for c in copies:
                c.wait_send()
        return wait

    wait = exchange("gx", mx, gx, xsend, xrecv, xs_sem, xr_sem)

    edge_lo = jnp.where(my == 0, 1.0, 0.0)
    edge_hi = jnp.where(my == gy - 1, 1.0, 0.0)
    for j in range(ny):
        gm, gp = yw[j], yw[j + 1]
        if j == 0:
            mass, link = 1.0 + edge_lo * gm, (1.0 - edge_lo) * gm
        else:
            mass, link = 1.0 + w * mass, w * link
        if j < ny - 1:
            ib = 1.0 / (mass + link + gp)
            w = gp * ib
            e = link * ib
            ye[j], yi[j], yw[j] = e, ib, w
            sig = e * mass if j == 0 else sig + e * mass
    mass = mass + edge_hi * yw[ny]
    split_send((link, mass, sig), ycs, gy, ly)
    wait_c = exchange("gy", my, gy, ycs, ycr, ycs_sem, ycr_sem)

    wait()

    def reduced_factor(recv, count):
        ws, ibs = [], []
        for i in range(count):
            total = recv[i, 1] + (recv[i + 1, 2] if i < count - 1 else 0.0)
            s = total if i == 0 else total + ws[-1] * s
            if i < count - 1:
                ib = 1.0 / (s + recv[i + 1, 0])
                ws.append(recv[i + 1, 0] * ib)
            else:
                ib = 1.0 / s
            ibs.append(ib)
        return ws, ibs

    def reduced_solve(ws, ibs, own, below, count, back):
        ds = []
        for i in range(count):
            d = own(i) + (below(i + 1) if i < count - 1 else 0.0)
            ds.append(d if i == 0 else d + ws[i - 1] * ds[-1])
        x = ds[-1] * ibs[-1]
        back[count - 1, 1] = x
        for i in range(count - 2, -1, -1):
            x = ds[i] * ibs[i] + ws[i] * x
            back[i, 1] = x
            back[i + 1, 0] = x
        back[0, 0] = jnp.zeros_like(x)

    ws, ibs = reduced_factor(xrecv, gx)
    reduced_solve(ws, ibs, lambda i: xrecv[i, 3], lambda i: xrecv[i, 4], gx, xback)
    wait = exchange("gx", mx, gx, xback, xgot, xbs_sem, xbr_sem)
    for step in (0, 1):
        zfactor(step)
    wait()

    low = joined([xgot[t, 0] for t in range(gx)])
    x = joined([xgot[t, 1] for t in range(gx)])
    for i in range(nx - 1, -1, -1):
        if i < nx - 1:
            x = xd[i] + xe[i] * low + xw[i] * x
        for h in range(2):
            rhs[h, pl.ds(i * ny, ny), :] = x[h * ny:(h + 1) * ny]

    for j in range(ny):
        d = joined([rhs[h, pl.ds(j, nx, stride=ny), :] for h in range(2)])
        dd = d if j == 0 else d + yw[j - 1] * dd
        if j < ny - 1:
            yd[j] = dd * yi[j]
            d1 = ye[j] * dd if j == 0 else d1 + ye[j] * dd
    split_send((dd, d1), yrs, gy, ly)
    wait = exchange("gy", my, gy, yrs, yrr, yrs_sem, yrr_sem)
    wait_c()
    ws, ibs = reduced_factor(ycr, gy)
    for i in range(gy):
        yfi[i] = ibs[i]
        if i < gy - 1:
            yfw[i] = ws[i]
    for step in (2, 3, 4):
        zfactor(step)
    wait()
    reduced_solve([yfw[i] for i in range(gy - 1)], [yfi[i] for i in range(gy)],
                  lambda i: yrr[i, 0], lambda i: yrr[i, 1], gy, yback)
    wait = exchange("gy", my, gy, yback, ygot, ybs_sem, ybr_sem)
    for step in (5, 6, 7):
        zfactor(step)
    wait()

    low = joined([ygot[t, 0] for t in range(gy)])
    x = joined([ygot[t, 1] for t in range(gy)])
    for j in range(ny - 1, -1, -1):
        if j < ny - 1:
            x = yd[j] + ye[j] * low + yw[j] * x
        for h in range(2):
            rhs[h, pl.ds(j, nx, stride=ny), :] = x[h * nx:(h + 1) * nx]

    for step in range(7):
        s = 1 << step
        for r in range(0, rows, block):
            at = pl.ds(r, block)
            d = [rhs[h, at, :] for h in range(2)]
            dp, dn = prev(d, s), nxt(d, s)
            for h in range(2):
                rhs[h, at, :] = d[h] + zfm[step, h, at, :] * dp[h] + zfp[step, h, at, :] * dn[h]
    for r in range(0, rows, block):
        at = pl.ds(r, block)
        d = [rhs[h, at, :] for h in range(2)]
        for h in range(2):
            rhs[h, at, :] = field[0, h, at, :] + (d[h] + zfm[7, h, at, :] * d[1 - h]) * zfp[7, h, at, :]
    stores = []
    for h in range(2):
        c = pltpu.make_async_copy(rhs.at[h], o_hbm.at[:, pl.ds(h * LANES, LANES)], out_sem.at[h])
        c.start()
        stores.append(c)
    for c in stores:
        c.wait()


def local(gx, gy, initial_warmth, energy_source_density, baseline_transport_coefficient):
    nx, ny, nz = initial_warmth.shape
    rows = nx * ny
    xr, yr = 2 * ny, 2 * nx
    lx, ly = xr // gx, yr // gy
    flat = [a.reshape(rows, nz) for a in (initial_warmth, energy_source_density, baseline_transport_coefficient)]

    def vm(*shape):
        return pltpu.VMEM(shape, jnp.float32)

    dma = pltpu.SemaphoreType.DMA
    out = pl.pallas_call(
        functools.partial(kernel, nx, ny, gx, gy, lx, ly),
        out_shape=jax.ShapeDtypeStruct((rows, nz), jnp.float32),
        in_specs=[pl.BlockSpec(memory_space=pl.ANY)] * 3,
        out_specs=pl.BlockSpec(memory_space=pl.ANY),
        scratch_shapes=[
            vm(2, 2, rows, LANES), vm(2, rows, LANES),
            vm(nx, xr, LANES), vm(nx, xr, LANES), vm(nx, xr, LANES),
            vm(ny, yr, LANES), vm(ny, yr, LANES), vm(ny + 1, yr, LANES), vm(ny, yr, LANES),
            vm(2, 2, 2, ny, LANES), vm(2, 2, 2, nx, LANES), vm(2, 2, 2, nx, LANES),
            vm(3, 2, rows, LANES), vm(8, 2, rows, LANES), vm(8, 2, rows, LANES),
            vm(gx, 5, lx, LANES), vm(gx, 5, lx, LANES), vm(gx, 2, lx, LANES), vm(gx, 2, lx, LANES),
            vm(gy, 3, ly, LANES), vm(gy, 3, ly, LANES), vm(gy, 2, ly, LANES), vm(gy, 2, ly, LANES),
            vm(gy, 2, ly, LANES), vm(gy, 2, ly, LANES),
            vm(gy, ly, LANES), vm(gy, ly, LANES),
            dma((3, 2)), dma((2,)), dma((4,)), dma((4,)),
            dma((gx,)), dma((gx,)), dma((gx,)), dma((gx,)),
            dma((gy,)), dma((gy,)), dma((gy,)), dma((gy,)), dma((gy,)), dma((gy,)),
        ],
        compiler_params=pltpu.CompilerParams(
            collective_id=0, has_side_effects=True, vmem_limit_bytes=40 * 1024 * 1024),
        name="adi_step",
    )(*flat)
    return out.reshape(nx, ny, nz)


def solution(mesh):
    spec = P("gx", "gy", None)
    return jax.shard_map(
        functools.partial(local, mesh.shape["gx"], mesh.shape["gy"]),
        mesh=mesh,
        in_specs=(spec, spec, spec),
        out_specs=spec,
        check_vma=False,
    )
```

```python
import functools

import jax
import jax.numpy as jnp
from jax import lax
from jax.experimental import pallas as pl
from jax.experimental.pallas import tpu as pltpu
from jax.sharding import PartitionSpec as P

MESH = pl.DeviceIdType.MESH
LANES = 128


def kernel(nx, ny, gx, gy, ly, u_hbm, s_hbm, k_hbm, o_hbm,
           field, rhs, xd, xe, xw, xi, yd, ye, yw, yi, xz, yz, hx, hys, hyr,
           zq, zfm, zfp,
           xcs, xcr, xrs, xrr, xred, xfw, xfi, xx, ycs, ycr, yrs, yrr, yback, ygot, yfw, yfi,
           in_sem, out_sem, hs_sem, hr_sem, xcs_sem, xcr_sem, xrs_sem, xrr_sem,
           ycs_sem, ycr_sem, yrs_sem, yrr_sem, ybs_sem, ybr_sem):
    rows = nx * ny
    mx = lax.axis_index("gx")
    my = lax.axis_index("gy")

    loads = []
    for a, (src, dst) in enumerate(((u_hbm, field.at[0]), (k_hbm, field.at[1]), (s_hbm, rhs))):
        for h in range(2):
            c = pltpu.make_async_copy(src.at[:, pl.ds(h * LANES, LANES)], dst.at[h], in_sem.at[a, h])
            c.start()
            loads.append(c)

    barrier = pltpu.get_barrier_semaphore()
    for o in range(1, gx):
        pl.semaphore_signal(barrier, inc=1, device_id={"gx": lax.rem(mx + o, gx)}, device_id_type=MESH)
    for o in range(1, gy):
        pl.semaphore_signal(barrier, inc=1, device_id={"gy": lax.rem(my + o, gy)}, device_id_type=MESH)

    for c in loads[:4]:
        c.wait()
    block = 32
    for r in range(0, rows, block):
        u = field[0, :, r:r + block, :]
        field[1, :, r:r + block, :] = field[1, :, r:r + block, :] * (1.0 + 0.5 * u * u)

    for q in range(2):
        for h in range(2):
            hys[0, q, h] = field[q, h, pl.ds(0, nx, stride=ny), :]
            hys[1, q, h] = field[q, h, pl.ds(ny - 1, nx, stride=ny), :]

    for c in loads[4:]:
        c.wait()

    lane = lax.broadcasted_iota(jnp.int32, (block, LANES), 1)

    def prev(a, s):
        if s == LANES:
            return a[1], a[0]
        p0, p1 = pltpu.roll(a[0], s, 1), pltpu.roll(a[1], s, 1)
        return p0, jnp.where(lane < s, p0, p1)

    def nxt(a, s):
        n0, n1 = pltpu.roll(a[0], LANES - s, 1), pltpu.roll(a[1], LANES - s, 1)
        return jnp.where(lane >= LANES - s, n1, n0), n1

    first, last = lane == 0, lane == LANES - 1

    for r in range(0, rows, block):
        at = pl.ds(r, block)
        u = [field[0, h, at, :] for h in range(2)]
        c = [field[1, h, at, :] for h in range(2)]
        up_, cp = prev(u, 1), prev(c, 1)
        un, cn = nxt(u, 1), nxt(c, 1)
        zero = jnp.zeros_like(lane, jnp.float32)
        up_, cp = [jnp.where(first, zero, up_[0]), up_[1]], [jnp.where(first, zero, cp[0]), cp[1]]
        un, cn = [un[0], jnp.where(last, zero, un[1])], [cn[0], jnp.where(last, zero, cn[1])]
        for h in range(2):
            gm, gp = 0.25 * (c[h] + cp[h]), 0.25 * (c[h] + cn[h])
            rhs[h, at, :] = rhs[h, at, :] + 2.0 * (gp * (un[h] - u[h]) - gm * (u[h] - up_[h]))
            if h == 0:
                zq[0, h, at, :] = jnp.where(first, zero, gm)
                zq[1, h, at, :] = gp
                zq[2, h, at, :] = jnp.where(first, 1.0 + gm, 1.0)
            else:
                zq[0, h, at, :] = gm
                zq[1, h, at, :] = jnp.where(last, zero, gp)
                zq[2, h, at, :] = jnp.where(last, 1.0 + gp, 1.0)

    def zfactor(step):
        s = 1 << step
        for r in range(0, rows, block):
            at = pl.ds(r, block)
            qm = [zq[0, h, at, :] for h in range(2)]
            qp = [zq[1, h, at, :] for h in range(2)]
            m = [zq[2, h, at, :] for h in range(2)]
            ib = [1.0 / (m[h] + (qm[h] + qp[h])) for h in range(2)]
            if s == LANES:
                fp0, fm1 = qp[0] * ib[1], qm[1] * ib[0]
                zfm[step, 0, at, :] = fp0
                zfm[step, 1, at, :] = fm1
                zfp[step, 0, at, :] = 1.0 / (m[0] + fp0 * m[1])
                zfp[step, 1, at, :] = 1.0 / (m[1] + fm1 * m[0])
                continue
            ip, inx = prev(ib, s), nxt(ib, s)
            mp, mn = prev(m, s), nxt(m, s)
            qmp, qpn = prev(qm, s), nxt(qp, s)
            for h in range(2):
                fm, fp = qm[h] * ip[h], qp[h] * inx[h]
                zfm[step, h, at, :] = fm
                zfp[step, h, at, :] = fp
                zq[0, h, at, :] = fm * qmp[h]
                zq[1, h, at, :] = fp * qpn[h]
                zq[2, h, at, :] = m[h] + (fm * mp[h] + fp * mn[h])

    def joined(parts):
        return jnp.concatenate(parts, axis=0)

    def xat(i):
        return pl.ds(i * ny, ny)

    def yat(j):
        return pl.ds(j, nx, stride=ny)

    def line(ref, at):
        return joined([ref[h, at, :] for h in range(2)])

    def put_line(ref, at, v):
        half = v.shape[0] // 2
        for h in range(2):
            ref[h, at, :] = v[h * half:(h + 1) * half]

    def split_send(values, buf, count, per):
        for q, v in enumerate(values):
            for t in range(count):
                buf[t, q] = v[t * per:(t + 1) * per]

    def inner(n, at, si, se, sw):
        u, c = line(field.at[0], at(0)), line(field.at[1], at(0))
        flux = None
        for i in range(n):
            if i < n - 1:
                un, cn = line(field.at[0], at(i + 1)), line(field.at[1], at(i + 1))
                gp = 0.25 * (c + cn)
                fp = 2.0 * (gp * (un - u))
                change = fp if flux is None else fp - flux
            else:
                change = -flux
            put_line(rhs, at(i), line(rhs, at(i)) + change)
            if i == 1:
                mass, link = 1.0, gm
            elif i > 1:
                mass, link = 1.0 + w * mass, w * link
            if 0 < i < n - 1:
                ib = 1.0 / (mass + link + gp)
                w, e = gp * ib, link * ib
                si[i], se[i], sw[i] = ib, e, w
                sig = 1.0 + e * mass if i == 1 else sig + e * mass
            if i < n - 1:
                flux, u, c, gm = fp, un, cn, gp
        return sig, link, mass

    def row_zero(mass_0, link, g):
        ib = 1.0 / (mass_0 + (link + g))
        w, e = link * ib, g * ib
        return ib, w, e, w * g, w * mass_0, e * mass_0

    def sides(n, at, recv):
        out = []
        for side, i in ((0, 0), (1, n - 1)):
            un, cn = [joined([recv[side, q, 0], recv[side, q, 1]]) for q in range(2)]
            g = 0.25 * (line(field.at[1], at(i)) + cn)
            put_line(rhs, at(i), line(rhs, at(i)) + 2.0 * (g * (un - line(field.at[0], at(i)))))
            out.append(g)
        return out

    def forward(n, at, si, se, sw, sd):
        dd = line(rhs, at(1))
        for i in range(1, n - 1):
            if i > 1:
                dd = line(rhs, at(i)) + sw[i - 1] * dd
            sd[i] = dd * si[i]
            d1 = se[i] * dd if i == 1 else d1 + se[i] * dd
        return line(rhs, at(0)) + d1, line(rhs, at(n - 1)) + sw[n - 2] * dd

    def backward(n, at, se, sw, sd, x0, xl):
        put_line(rhs, at(n - 1), xl)
        x = xl
        for i in range(n - 2, 0, -1):
            x = sd[i] + se[i] * x0 + sw[i] * x
            put_line(rhs, at(i), x)
        put_line(rhs, at(0), x0)

    def halo(axis, me, count, src_first, src_last, recv, base):
        down = pltpu.make_async_remote_copy(
            src_ref=src_first, dst_ref=recv.at[1], send_sem=hs_sem.at[base], recv_sem=hr_sem.at[base],
            device_id={axis: lax.rem(me + count - 1, count)}, device_id_type=MESH)
        up = pltpu.make_async_remote_copy(
            src_ref=src_last, dst_ref=recv.at[0], send_sem=hs_sem.at[base + 1], recv_sem=hr_sem.at[base + 1],
            device_id={axis: lax.rem(me + 1, count)}, device_id_type=MESH)

        @pl.when(me > 0)
        def _():
            down.start()

        @pl.when(me < count - 1)
        def _():
            up.start()

        @pl.when(me == 0)
        def _():
            recv[0] = jnp.zeros(recv.shape[1:], jnp.float32)

        @pl.when(me == count - 1)
        def _():
            recv[1] = jnp.zeros(recv.shape[1:], jnp.float32)

        def wait():
            @pl.when(me > 0)
            def _():
                down.wait_send()
                up.wait_recv()

            @pl.when(me < count - 1)
            def _():
                up.wait_send()
                down.wait_recv()
        return wait

    def exchange(axis, me, count, src, dst, send_sem, recv_sem):
        copies = []
        for o in range(1, count):
            peer = lax.rem(me + o, count)
            c = pltpu.make_async_remote_copy(
                src_ref=src.at[peer], dst_ref=dst.at[me], send_sem=send_sem.at[o], recv_sem=recv_sem.at[o],
                device_id={axis: peer}, device_id_type=MESH)
            c.start()
            copies.append(c)
        dst[me] = src[me]

        def wait():
            for o in range(1, count):
                origin = lax.rem(me + count - o, count)
                c = pltpu.make_async_remote_copy(
                    src_ref=src.at[origin], dst_ref=dst.at[origin], send_sem=send_sem.at[o],
                    recv_sem=recv_sem.at[o], device_id={axis: origin}, device_id_type=MESH)
                c.wait_recv()
            for c in copies:
                c.wait_send()
        return wait

    def gather(axis, me, count, src, dst, send_sem, recv_sem):
        copies = []
        for o in range(1, count):
            c = pltpu.make_async_remote_copy(
                src_ref=src, dst_ref=dst.at[me], send_sem=send_sem.at[o], recv_sem=recv_sem.at[o],
                device_id={axis: lax.rem(me + o, count)}, device_id_type=MESH)
            c.start()
            copies.append(c)
        dst[me] = src[...]

        def wait():
            for o in range(1, count):
                origin = lax.rem(me + count - o, count)
                c = pltpu.make_async_remote_copy(
                    src_ref=src, dst_ref=dst.at[origin], send_sem=send_sem.at[o],
                    recv_sem=recv_sem.at[o], device_id={axis: origin}, device_id_type=MESH)
                c.wait_recv()
            for c in copies:
                c.wait_send()
        return wait

    def reduced_factor(recv, count):
        ws, ibs = [], []
        for i in range(count):
            total = recv[i, 1] + (recv[i + 1, 2] if i < count - 1 else 0.0)
            s = total if i == 0 else total + ws[-1] * s
            if i < count - 1:
                ib = 1.0 / (s + recv[i + 1, 0])
                ws.append(recv[i + 1, 0] * ib)
            else:
                ib = 1.0 / s
            ibs.append(ib)
        return ws, ibs

    def reduced_solve(ws, ibs, own, below, count, back):
        ds = []
        for i in range(count):
            d = own(i) + (below(i + 1) if i < count - 1 else 0.0)
            ds.append(d if i == 0 else d + ws[i - 1] * ds[-1])
        x = ds[-1] * ibs[-1]
        back[count - 1, 1] = x
        for i in range(count - 2, -1, -1):
            x = ds[i] * ibs[i] + ws[i] * x
            back[i, 1] = x
            back[i + 1, 0] = x
        back[0, 0] = jnp.zeros_like(x)

    x_mass_0, x_link, x_mass = inner(nx, xat, xi, xe, xw)
    xcs[0], xcs[1], xcs[2] = x_mass_0, x_link, x_mass
    xcs[3], xcs[4] = line(field.at[1], xat(0)), line(field.at[1], xat(nx - 1))

    pl.semaphore_wait(barrier, gx + gy - 2)

    wait_y = halo("gy", my, gy, hys.at[0], hys.at[1], hyr, 0)
    wait_x = halo("gx", mx, gx, field.at[:, :, pl.ds(0, ny), :],
                  field.at[:, :, pl.ds(rows - ny, ny), :], hx, 2)

    wait_xc = gather("gx", mx, gx, xcs, xcr, xcs_sem, xcr_sem)
    y_mass_0, y_link, y_mass = inner(ny, yat, yi, ye, yw)

    wait_y()
    y_low, y_high = sides(ny, yat, hyr)
    wait_x()
    x_low, x_high = sides(nx, xat, hx)

    own_lo = jnp.where(mx == 0, 1.0, 0.0)
    x_ib, x_w, x_e, _, _, _ = row_zero(x_mass_0 + own_lo * x_low, x_link, (1.0 - own_lo) * x_low)
    d0, dl = forward(nx, xat, xi, xe, xw, xd)
    xrs[0], xrs[1] = dl + x_w * d0, x_e * d0
    wait = gather("gx", mx, gx, xrs, xrr, xrs_sem, xrr_sem)
    x_d = d0 * x_ib

    own_lo = jnp.where(my == 0, 1.0, 0.0)
    own_hi = jnp.where(my == gy - 1, 1.0, 0.0)
    mass_0 = y_mass_0 + own_lo * y_low
    y_ib, y_w, y_e, link, more, sig = row_zero(mass_0, y_link, (1.0 - own_lo) * y_low)
    split_send((link, (y_mass + more) + own_hi * y_high, sig), ycs, gy, ly)
    wait_c = exchange("gy", my, gy, ycs, ycr, ycs_sem, ycr_sem)
    yz[0], yz[1], yz[2] = y_ib, y_w, y_e
    xz[0], xz[1], xz[2] = x_d, x_w, x_e

    wait_xc()
    for t in range(gx):
        m0, ml = xcr[t, 0], xcr[t, 2]
        if t == 0:
            m0 = m0 + 0.25 * xcr[t, 3]
            g = jnp.zeros_like(m0)
        else:
            g = 0.25 * (xcr[t - 1, 4] + xcr[t, 3])
        if t == gx - 1:
            ml = ml + 0.25 * xcr[t, 4]
        _, _, _, link, more, sig = row_zero(m0, xcr[t, 1], g)
        xred[t, 0], xred[t, 1], xred[t, 2] = link, ml + more, sig
    ws, ibs = reduced_factor(xred, gx)
    for i in range(gx):
        xfi[i] = ibs[i]
        if i < gx - 1:
            xfw[i] = ws[i]
    for step in (0, 1, 2):
        zfactor(step)
    wait()
    ws, ibs = [xfw[i] for i in range(gx - 1)], [xfi[i] for i in range(gx)]
    ds = []
    for i in range(gx):
        d = xrr[i, 0] + (xrr[i + 1, 1] if i < gx - 1 else 0.0)
        ds.append(d if i == 0 else d + ws[i - 1] * ds[-1])
    x = ds[-1] * ibs[-1]
    xx[gx] = x
    for i in range(gx - 2, -1, -1):
        x = ds[i] * ibs[i] + ws[i] * x
        xx[i + 1] = x
    xx[0] = jnp.zeros_like(x)

    low, xl = xx[mx], xx[mx + 1]
    backward(nx, xat, xe, xw, xd, xz[0] + xz[2] * low + xz[1] * xl, xl)

    d0, dl = forward(ny, yat, yi, ye, yw, yd)
    split_send((dl + yz[1] * d0, yz[2] * d0), yrs, gy, ly)
    wait = exchange("gy", my, gy, yrs, yrr, yrs_sem, yrr_sem)
    yz[3] = d0 * yz[0]
    wait_c()
    ws, ibs = reduced_factor(ycr, gy)
    for i in range(gy):
        yfi[i] = ibs[i]
        if i < gy - 1:
            yfw[i] = ws[i]
    for step in (3, 4, 5):
        zfactor(step)
    wait()
    reduced_solve([yfw[i] for i in range(gy - 1)], [yfi[i] for i in range(gy)],
                  lambda i: yrr[i, 0], lambda i: yrr[i, 1], gy, yback)
    wait = exchange("gy", my, gy, yback, ygot, ybs_sem, ybr_sem)
    for step in (6, 7):
        zfactor(step)
    wait()
    low = joined([ygot[t, 0] for t in range(gy)])
    xl = joined([ygot[t, 1] for t in range(gy)])
    backward(ny, yat, ye, yw, yd, yz[3] + yz[2] * low + yz[1] * xl, xl)

    for step in range(7):
        s = 1 << step
        for r in range(0, rows, block):
            at = pl.ds(r, block)
            d = [rhs[h, at, :] for h in range(2)]
            dp, dn = prev(d, s), nxt(d, s)
            for h in range(2):
                rhs[h, at, :] = d[h] + zfm[step, h, at, :] * dp[h] + zfp[step, h, at, :] * dn[h]
    for r in range(0, rows, block):
        at = pl.ds(r, block)
        d = [rhs[h, at, :] for h in range(2)]
        for h in range(2):
            rhs[h, at, :] = field[0, h, at, :] + (d[h] + zfm[7, h, at, :] * d[1 - h]) * zfp[7, h, at, :]
    stores = []
    for h in range(2):
        c = pltpu.make_async_copy(rhs.at[h], o_hbm.at[:, pl.ds(h * LANES, LANES)], out_sem.at[h])
        c.start()
        stores.append(c)
    for c in stores:
        c.wait()


def local(gx, gy, initial_warmth, energy_source_density, baseline_transport_coefficient):
    nx, ny, nz = initial_warmth.shape
    rows = nx * ny
    xr, yr = 2 * ny, 2 * nx
    ly = yr // gy
    flat = [a.reshape(rows, nz) for a in (initial_warmth, energy_source_density, baseline_transport_coefficient)]

    def vm(*shape):
        return pltpu.VMEM(shape, jnp.float32)

    dma = pltpu.SemaphoreType.DMA
    out = pl.pallas_call(
        functools.partial(kernel, nx, ny, gx, gy, ly),
        out_shape=jax.ShapeDtypeStruct((rows, nz), jnp.float32),
        in_specs=[pl.BlockSpec(memory_space=pl.ANY)] * 3,
        out_specs=pl.BlockSpec(memory_space=pl.ANY),
        scratch_shapes=[
            vm(2, 2, rows, LANES), vm(2, rows, LANES),
            vm(nx, xr, LANES), vm(nx, xr, LANES), vm(nx, xr, LANES), vm(nx, xr, LANES),
            vm(ny, yr, LANES), vm(ny, yr, LANES), vm(ny, yr, LANES), vm(ny, yr, LANES),
            vm(3, xr, LANES), vm(4, yr, LANES),
            vm(2, 2, 2, ny, LANES), vm(2, 2, 2, nx, LANES), vm(2, 2, 2, nx, LANES),
            vm(3, 2, rows, LANES), vm(8, 2, rows, LANES), vm(8, 2, rows, LANES),
            vm(5, xr, LANES), vm(gx, 5, xr, LANES), vm(2, xr, LANES), vm(gx, 2, xr, LANES),
            vm(gx, 3, xr, LANES), vm(gx, xr, LANES), vm(gx, xr, LANES), vm(gx + 1, xr, LANES),
            vm(gy, 3, ly, LANES), vm(gy, 3, ly, LANES), vm(gy, 2, ly, LANES), vm(gy, 2, ly, LANES),
            vm(gy, 2, ly, LANES), vm(gy, 2, ly, LANES),
            vm(gy, ly, LANES), vm(gy, ly, LANES),
            dma((3, 2)), dma((2,)), dma((4,)), dma((4,)),
            dma((gx,)), dma((gx,)), dma((gx,)), dma((gx,)),
            dma((gy,)), dma((gy,)), dma((gy,)), dma((gy,)), dma((gy,)), dma((gy,)),
        ],
        compiler_params=pltpu.CompilerParams(
            collective_id=0, has_side_effects=True, vmem_limit_bytes=60 * 1024 * 1024),
        name="adi_step",
    )(*flat)
    return out.reshape(nx, ny, nz)


def solution(mesh):
    spec = P("gx", "gy", None)
    return jax.shard_map(
        functools.partial(local, mesh.shape["gx"], mesh.shape["gy"]),
        mesh=mesh,
        in_specs=(spec, spec, spec),
        out_specs=spec,
        check_vma=False,
    )
```
